32 devices in a mesh: cfg: 2 (over x), prow: 16 (over z, y, core).
Axes of the slice: x: 2, y: 2, z: 4, core: 2. Of those that a mesh axis runs over, the one named last changes fastest.
Arguments:
- top_panels: float32 [3072, 1536], P(('cfg', 'prow')), parts along dimension 0, may hold values from -0.15625 to 0.15625
- top_inverse: float32 [12, 256, 256], P('cfg'), parts along dimension 0, as said below
- pattern: int32 [64, 3], P('prow'), may hold values from 0 to 5, all different within a row
- child_blocks: float32 [128, 3, 256, 256], P(('cfg', 'prow')), parts along dimension 0, may hold values from -0.21875 to 0.21875
- child_inverse: float32 [128, 256, 256], P(('cfg', 'prow')), parts along dimension 0, as said below
Outputs:
- top_var: float32 [3072], P(('cfg', 'prow')), parts along dimension 0
- child_var: float32 [128, 256], P(('cfg', 'prow')), parts along dimension 0
The draws below stay inside these ranges and needn't reach their ends.
There are 2 independent parts, one for each index of `cfg`. The reference program is written for one: setup_inputs(seed, part) draws one part's arguments, and reference() takes and returns one part's arrays. A program takes and returns all parts, laid end to end along the dimension named above; an argument that names none is the same for every part. Nothing has to cross between parts.
Inputs may be any that keep to these rules, and one draw needn't show every extreme that they name: `pattern`: each row names 3 different top supernodes; every top supernode is named by some row. `top_inverse`: each block is lower triangular with a positive diagonal. `child_inverse`: each block is lower triangular with a positive diagonal.
All inputs are finite; a program needn't handle non-finite values.
Results may differ from the reference program's by a relative error of at most 0.0001.
Values sent between devices are 32-bit elements; how exact they have to be, the bound alone decides.
A program may use at most 128 MiB of HBM per device.

```python
import jax
import jax.numpy as jnp
from jax import lax

NB = 256
NT = 6
PAT = 3
MT = 1536
CHILDREN = 64


def lower_factor(key, count, width, scale, low, high):
    first, second = jax.random.split(key)
    strict = jax.random.normal(first, (count, width, width), jnp.float32) * (scale / width ** 0.5)
    diag_part = jax.random.uniform(second, (count, width), jnp.float32, minval=low, maxval=high)
    return jnp.tril(strict, -1) + diag_part[:, :, None] * jnp.eye(width, dtype=jnp.float32)


def draw_top_inverse(key, part):
    key = jax.random.fold_in(key, 11)
    return lower_factor(key, NT, NB, 0.6, 0.6, 1.5)


def draw_child_inverse(key, part):
    key = jax.random.fold_in(key, 23)
    return lower_factor(key, CHILDREN, NB, 0.6, 0.6, 1.5)


def block_levels(stream_key, shape, pieces, low, high):
    gain = 1.0
    for axis_at, blocks in pieces:
        draws = jax.random.uniform(jax.random.fold_in(jax.random.fold_in(stream_key, 6), axis_at), (blocks,), jnp.float32, low / len(pieces), high / len(pieces))
        gain = gain * jnp.repeat(jnp.exp(draws), shape[axis_at] // blocks).reshape((-1,) + (1,) * (len(shape) - 1 - axis_at))
    return gain


def choose_distinct(rng, rows, count, top, lift):
    ranking = jax.random.permutation(jax.random.fold_in(rng, 1), count)
    pull = ranking
    for power in range(3):
        pull = pull * pull // count
    pull = pull * lift // count
    lots = jax.random.randint(jax.random.fold_in(rng, 2), (rows, count), 0, 4096) + pull
    fixed_rows = jax.random.permutation(jax.random.fold_in(rng, 3), rows)[jnp.arange(count) % rows]
    lots = jnp.where(jnp.arange(rows)[:, None] == fixed_rows[None, :], 1 << 14, lots)
    priority = lots * count + jnp.arange(count)
    return lax.top_k(priority.astype(jnp.int32), top)[1].astype(jnp.int32)


def bell_draw(key, shape, spread, most, shards=(), held_as=jnp.bfloat16):
    result = jax.random.normal(key, shape, jnp.float32) * spread
    if len(shards) > 0:
        result = block_levels(key, shape, shards, -0.22, 0.18) * result
    return jnp.clip(result, min=-most, max=most).astype(held_as)


def setup_inputs(seed: int = 0, part: int = 0) -> dict:
    keys = jax.random.split(jax.random.key(seed), 6)
    own_keys = jax.random.split(jax.random.fold_in(keys[5], part), 6)
    top_panels = bell_draw(own_keys[0], (MT, MT), MT ** -0.5, 0.15625, ((0, 16),), jnp.float32)
    top_inverse = draw_top_inverse(jax.random.fold_in(jax.random.fold_in(keys[5], part), 71), part)
    pattern = choose_distinct(keys[2], CHILDREN, NT, PAT, 0)
    child_blocks = bell_draw(own_keys[3], (CHILDREN, PAT, NB, NB), (PAT * NB) ** -0.5, 0.21875, ((0, 16),), jnp.float32)
    child_inverse = draw_child_inverse(jax.random.fold_in(jax.random.fold_in(keys[5], part), 71), part)
    return {"top_panels": top_panels, "top_inverse": top_inverse, "pattern": pattern, "child_blocks": child_blocks, "child_inverse": child_inverse}


def exact_dot(left, right):
    return jnp.dot(left, right, precision=lax.Precision.HIGHEST, preferred_element_type=jnp.float32)


def top_recursion(panels, inverse):
    count, width = inverse.shape[0], inverse.shape[1]
    order = count * width
    sigma = jnp.zeros((order, order), jnp.float32)
    for k in reversed(range(count)):
        start = k * width
        end = start + width
        factor = inverse[k]
        block = exact_dot(factor.T, factor)
        if end < order:
            scaled = exact_dot(panels[end:, start:end], factor)
            column = -exact_dot(sigma[end:, end:], scaled)
            block = block - exact_dot(scaled.T, column)
            sigma = sigma.at[end:, start:end].set(column)
            sigma = sigma.at[start:end, end:].set(column.T)
        sigma = sigma.at[start:end, start:end].set(block)
    return sigma


def child_variance(sigma, blocks, factor, picks):
    count = sigma.shape[0] // factor.shape[0]
    width = factor.shape[0]
    grid = sigma.reshape(count, width, count, width)
    chosen = jnp.take(jnp.take(grid, picks, axis=0), picks, axis=2)
    scaled = jnp.einsum("iab,bn->ian", blocks, factor, precision=lax.Precision.HIGHEST)
    coupled = jnp.einsum("iajb,jbn->ian", chosen, scaled, precision=lax.Precision.HIGHEST)
    return jnp.sum(factor * factor, axis=0) + jnp.sum(scaled * coupled, axis=(0, 1))


def reference(top_panels, top_inverse, pattern, child_blocks, child_inverse):
    sigma = top_recursion(top_panels, top_inverse)
    top_var = jnp.diagonal(sigma)

    def one(items):
        return child_variance(sigma, items[0], items[1], items[2])

    child_var = lax.map(one, (child_blocks, child_inverse, pattern))
    return top_var, child_var
```

```python
import functools

import jax
import jax.numpy as jnp
from jax import lax
from jax.experimental import pallas as pl
from jax.experimental.pallas import tpu as pltpu
from jax.sharding import PartitionSpec as P

F32 = jnp.float32
BF16 = jnp.bfloat16
MESH = pl.DeviceIdType.MESH


def split(x):
    high = x.astype(BF16)
    low = (x - high.astype(F32)).astype(BF16)
    return high, low


def mm(a, b):
    return jnp.dot(a, b, preferred_element_type=F32)


def mm3(ah, al, bh, bl):
    return mm(ah, bh) + mm(ah, bl) + mm(al, bh)


def kernel(
    n, nt, nb, rows, kids, links,
    panels_hbm, winv_hbm, pat, blocks_hbm, kinv_hbm,
    top_out, kid_out,
    pan, winv, blocks, kinv, w_h, w_l, wtw, sig_h, sig_l, u_h, u_l, kid_h, kid_f,
    own_sem, load_sem, recv_sem, up_sem, down_sem, y_sem, core_sem,
):
    cfg = lax.axis_index("cfg")
    me = lax.axis_index("prow")
    nz = n // 4
    z = me // 4
    y = (me // 2) % 2
    c = me % 2

    def index(zo, yo, co):
        return zo * 4 + yo * 2 + co

    y_peer = index(z, 1 - y, c)
    core_peer = index(z, y, 1 - c)
    below = index(jnp.maximum(z - 1, 0), y, c)
    above = index(jnp.minimum(z + 1, nz - 1), y, c)

    def needed(owner, k):
        return owner * rows + rows - 1 >= (k + 1) * nb

    own_copies = []
    for k in reversed(range(nt - 1)):
        copy = pltpu.make_async_copy(
            panels_hbm.at[:, k * nb:(k + 1) * nb],
            pan.at[k, pl.ds(me * rows, rows), :],
            own_sem.at[k],
        )
        copy.start()
        own_copies.append(copy)
    load_w = pltpu.make_async_copy(winv_hbm, winv, load_sem.at[0])
    load_v = pltpu.make_async_copy(kinv_hbm, kinv, load_sem.at[1])
    load_b = pltpu.make_async_copy(blocks_hbm, blocks, load_sem.at[2])
    load_w.start()
    load_v.start()
    load_b.start()

    barrier = pltpu.get_barrier_semaphore()
    for peer in (y_peer, core_peer):
        pl.semaphore_signal(barrier, inc=1, device_id=(cfg, peer), device_id_type=MESH)

    @pl.when(z > 0)
    def _():
        pl.semaphore_signal(barrier, inc=1, device_id=(cfg, below), device_id_type=MESH)

    @pl.when(z < nz - 1)
    def _():
        pl.semaphore_signal(barrier, inc=1, device_id=(cfg, above), device_id_type=MESH)

    peers = 2 + (z > 0).astype(jnp.int32) + (z < nz - 1).astype(jnp.int32)
    pl.semaphore_wait(barrier, peers)

    def piece(owner, k, peer, sem):
        part = pan.at[k, pl.ds(owner * rows, rows), :]
        return pltpu.make_async_remote_copy(
            src_ref=part, dst_ref=part, send_sem=sem, recv_sem=recv_sem.at[k, owner],
            device_id=(cfg, peer), device_id_type=MESH,
        )

    def recv(owner, k):
        piece(owner, k, core_peer, core_sem.at[k, 0, 0]).wait_recv()

    def column_copies(zo, k):
        owner = index(zo, y, c)
        return (
            (jnp.logical_and(zo >= z, z > 0), piece(owner, k, below, down_sem.at[k, zo])),
            (jnp.logical_and(zo <= z, z < nz - 1), piece(owner, k, above, up_sem.at[k, zo])),
            (None, piece(owner, k, y_peer, y_sem.at[k, zo])),
            (None, piece(owner, k, core_peer, core_sem.at[k, 0, zo])),
        )

    def for_column(zo, k, act):
        for cond, copy in column_copies(zo, k):
            if cond is None:
                act(copy)
            else:
                pl.when(cond)(functools.partial(act, copy))

    def start(copy):
        copy.start()

    def done(copy):
        copy.wait_send()

    def guarded(zo, yo, k, act):
        inside = jnp.logical_and(zo >= 0, zo < nz)
        pl.when(jnp.logical_and(inside, needed(index(zo, yo, c), k)))(act)

    def relay(k):
        def from_line(zo):
            def act():
                recv(index(zo, y, c), k)
                for_column(zo, k, start)
            guarded(zo, y, k, act)

        def from_y(zo):
            def act():
                owner = index(zo, 1 - y, c)
                recv(owner, k)
                piece(owner, k, core_peer, core_sem.at[k, 1, zo]).start()
            guarded(zo, 1 - y, k, act)

        def step(d, carry):
            from_line(z + d)
            from_line(z - d)
            @pl.when(d == 1)
            def _():
                from_y(z)

            @pl.when(d > 1)
            def _():
                from_y(z + d - 1)
                from_y(z - d + 1)
            return carry

        lax.fori_loop(1, nz, step, 0)
        from_y(z + nz - 1)
        from_y(z - nz + 1)

    def core_wait(k):
        def step(t, carry):
            owner = t * 2 + (1 - c)
            pl.when(needed(owner, k))(lambda: recv(owner, k))
            return carry
        lax.fori_loop(0, n // 2, step, 0)

    for copy, k in zip(own_copies, reversed(range(nt - 1))):
        copy.wait()

        @pl.when(needed(me, k))
        def _(k=k):
            for_column(z, k, start)

    load_w.wait()

    def prepare(k, carry):
        wh, wl = split(winv[k])
        w_h[k] = wh
        w_l[k] = wl
        th, tl = split(winv[k].T)
        wtw[k] = mm3(th, tl, wh, wl)
        return carry

    def kid_prepare(kid):
        vh, vl = split(kinv[kid])

        def step(i, carry):
            bh, bl = split(blocks[kid, i])
            value = mm3(bh, bl, vh, vl)
            high = value.astype(BF16)
            kid_h[kid, i] = high
            kid_f[kid, i] = 2.0 * value - high.astype(F32)
            return carry
        lax.fori_loop(0, links, step, 0)

    eye = (
        lax.broadcasted_iota(jnp.int32, (nb, nb), 0)
        == lax.broadcasted_iota(jnp.int32, (nb, nb), 1)
    )

    def set_diagonal(k, value):
        sig_h[k, k], sig_l[k, k] = split(value)
        top_out[k:k + 1, :] = jnp.sum(jnp.where(eye, value, 0.0), axis=0, keepdims=True)

    def column(k):
        after = range(k + 1, nt)

        def scale(r, carry):
            lh, ll = split(pan[k, pl.ds(r * nb, nb), :])
            value = mm3(lh, ll, w_h[k], w_l[k])
            u_h[r], u_l[r] = split(value)
            return carry
        lax.fori_loop(k + 1, nt, scale, 0)

        def row(i):
            total = None
            for j in after:
                term = mm3(sig_h[i, j], sig_l[i, j], u_h[j], u_l[j])
                total = term if total is None else total + term
            return total

        def fill(i, carry):
            value = -row(i)
            sig_h[i, k], sig_l[i, k] = split(value)
            sig_h[k, i], sig_l[k, i] = split(value.T)
            return carry
        lax.fori_loop(k + 1, nt, fill, 0)
        set_diagonal(k, wtw[k] - row(k))

    lax.fori_loop(0, nt, prepare, 0)
    set_diagonal(nt - 1, wtw[nt - 1])
    load_v.wait()
    load_b.wait()
    todo = list(range(kids))
    for k in reversed(range(nt - 1)):
        relay(k)
        if k + 1 < nt - 1:
            core_wait(k + 1)
            column(k + 1)
        if todo and k > 0:
            kid_prepare(todo.pop(0))
    for kid in todo:
        kid_prepare(kid)
    core_wait(0)
    column(0)

    def kid_finish(kid, carry):
        total = jnp.sum(kinv[kid] * kinv[kid], axis=0, keepdims=True)
        for i in range(links):
            coupled = None
            for j in range(links):
                bi, bj = pat[kid, i], pat[kid, j]
                term = mm(sig_h[bi, bj], kid_h[kid, j]) + mm(sig_l[bi, bj], kid_h[kid, j])
                coupled = term if coupled is None else coupled + term
            total = total + jnp.sum(kid_f[kid, i] * coupled, axis=0, keepdims=True)
        kid_out[pl.ds(kid, 1), :] = total
        return carry
    lax.fori_loop(0, kids, kid_finish, 0)

    for k in range(nt - 1):
        def finish(zo, carry, k=k):
            pl.when(needed(index(zo, y, c), k))(lambda: for_column(zo, k, done))

            @pl.when(needed(index(zo, 1 - y, c), k))
            def _():
                piece(index(zo, 1 - y, c), k, core_peer, core_sem.at[k, 1, zo]).wait_send()
            return carry
        lax.fori_loop(0, nz, finish, 0)


def local(n, top_panels, top_inverse, pattern, child_blocks, child_inverse):
    rows = top_panels.shape[0]
    nt, nb = top_inverse.shape[:2]
    kids, links = child_blocks.shape[:2]
    nz = n // 4
    dma = pltpu.SemaphoreType.DMA
    hbm = pl.BlockSpec(memory_space=pl.ANY)
    vmem = pl.BlockSpec(memory_space=pltpu.VMEM)
    diagonal, child_var = pl.pallas_call(
        functools.partial(kernel, n, nt, nb, rows, kids, links),
        out_shape=(
            jax.ShapeDtypeStruct((nt, nb), F32),
            jax.ShapeDtypeStruct((kids, nb), F32),
        ),
        in_specs=[hbm, hbm, pl.BlockSpec(memory_space=pltpu.SMEM), hbm, hbm],
        out_specs=(vmem, vmem),
        scratch_shapes=[
            pltpu.VMEM((nt - 1, nt * nb, nb), F32),
            pltpu.VMEM((nt, nb, nb), F32),
            pltpu.VMEM((kids, links, nb, nb), F32),
            pltpu.VMEM((kids, nb, nb), F32),
            pltpu.VMEM((nt, nb, nb), BF16),
            pltpu.VMEM((nt, nb, nb), BF16),
            pltpu.VMEM((nt, nb, nb), F32),
            pltpu.VMEM((nt, nt, nb, nb), BF16),
            pltpu.VMEM((nt, nt, nb, nb), BF16),
            pltpu.VMEM((nt, nb, nb), BF16),
            pltpu.VMEM((nt, nb, nb), BF16),
            pltpu.VMEM((kids, links, nb, nb), BF16),
            pltpu.VMEM((kids, links, nb, nb), F32),
            dma((nt - 1,)),
            dma((3,)),
            dma((nt - 1, n)),
            dma((nt - 1, nz)),
            dma((nt - 1, nz)),
            dma((nt - 1, nz)),
            dma((nt - 1, 2, nz)),
        ],
        compiler_params=pltpu.CompilerParams(
            collective_id=0, has_side_effects=True, vmem_limit_bytes=52 * 1024 * 1024,
        ),
    )(top_panels, top_inverse, pattern, child_blocks, child_inverse)
    first = lax.axis_index("prow") * rows
    top_var = lax.dynamic_slice_in_dim(diagonal.reshape(nt * nb), first, rows)
    return top_var, child_var


def solution(mesh):
    return jax.shard_map(
        functools.partial(local, mesh.shape["prow"]),
        mesh=mesh,
        in_specs=(
            P(("cfg", "prow"), None),
            P("cfg", None, None),
            P("prow", None),
            P(("cfg", "prow"), None, None, None),
            P(("cfg", "prow"), None, None),
        ),
        out_specs=(P(("cfg", "prow")), P(("cfg", "prow"), None)),
        check_vma=False,
    )
```

```python
import functools

import jax
import jax.numpy as jnp
from jax import lax
from jax.experimental import pallas as pl
from jax.experimental.pallas import tpu as pltpu
from jax.sharding import PartitionSpec as P

F32 = jnp.float32
BF16 = jnp.bfloat16
MESH = pl.DeviceIdType.MESH


def split(x):
    high = x.astype(BF16)
    low = (x - high.astype(F32)).astype(BF16)
    return high, low


def mm(a, b):
    return jnp.dot(a, b, preferred_element_type=F32)


def mm3(ah, al, bh, bl):
    return mm(ah, bh) + mm(ah, bl) + mm(al, bh)


def kernel(
    n, nt, nb, rows, kids, links,
    panels_hbm, winv_hbm, pat, blocks_hbm, kinv_hbm,
    top_out, kid_out,
    pan, winv, blocks, kinv, w_h, w_l, wtw, sig_h, sig_l, u_h, u_l, kid_h, kid_f,
    own_sem, load_sem, recv_sem, line_sem, down_sem, y_sem, core_sem,
):
    cfg = lax.axis_index("cfg")
    me = lax.axis_index("prow")
    nz = n // 4
    z = me // 4
    y = (me // 2) % 2
    c = me % 2

    def index(zo, yo, co):
        return zo * 4 + yo * 2 + co

    y_peer = index(z, 1 - y, c)
    core_peer = index(z, y, 1 - c)
    def needed(owner, k):
        return owner * rows + rows - 1 >= (k + 1) * nb

    own_copies = []
    for k in reversed(range(nt - 1)):
        copy = pltpu.make_async_copy(
            panels_hbm.at[:, k * nb:(k + 1) * nb],
            pan.at[k, pl.ds(me * rows, rows), :],
            own_sem.at[k],
        )
        copy.start()
        own_copies.append(copy)
    load_w = pltpu.make_async_copy(winv_hbm, winv, load_sem.at[0])
    load_v = pltpu.make_async_copy(kinv_hbm, kinv, load_sem.at[1])
    load_b = pltpu.make_async_copy(blocks_hbm, blocks, load_sem.at[2])
    load_w.start()
    load_v.start()
    load_b.start()

    barrier = pltpu.get_barrier_semaphore()
    for peer in (y_peer, core_peer):
        pl.semaphore_signal(barrier, inc=1, device_id=(cfg, peer), device_id_type=MESH)

    def greet(zo, carry):
        @pl.when(zo != z)
        def _():
            pl.semaphore_signal(
                barrier, inc=1, device_id=(cfg, index(zo, y, c)), device_id_type=MESH
            )
        return carry
    lax.fori_loop(0, nz, greet, 0)
    pl.semaphore_wait(barrier, nz + 1)

    def piece(owner, k, peer, sem):
        part = pan.at[k, pl.ds(owner * rows, rows), :]
        return pltpu.make_async_remote_copy(
            src_ref=part, dst_ref=part, send_sem=sem, recv_sem=recv_sem.at[k, owner],
            device_id=(cfg, peer), device_id_type=MESH,
        )

    def recv(owner, k):
        piece(owner, k, core_peer, core_sem.at[k, 0, 0]).wait_recv()

    def for_own(k, act):
        def to_line(zt):
            @pl.when(jnp.logical_and(zt != z, jnp.logical_or(zt > 0, z < 2)))
            def _():
                act(piece(me, k, index(zt, y, c), line_sem.at[k, zt]))

        def step(d, carry):
            pl.when(z - d >= 0)(lambda: to_line(z - d))
            pl.when(z + d < nz)(lambda: to_line(z + d))
            return carry
        lax.fori_loop(1, nz, step, 0)

    def for_column(zo, k, act):
        owner = index(zo, y, c)
        @pl.when(jnp.logical_and(z == 1, zo > 1))
        def _():
            act(piece(owner, k, index(0, y, c), down_sem.at[k, zo]))
        act(piece(owner, k, y_peer, y_sem.at[k, zo]))
        act(piece(owner, k, core_peer, core_sem.at[k, 0, zo]))

    def start(copy):
        copy.start()

    def done(copy):
        copy.wait_send()

    def highest(owner):
        return (owner * rows + rows - 1) // nb - 1

    def guarded(zo, yo, s, act):
        owner = index(zo, yo, c)
        inside = jnp.logical_and(zo >= 0, zo < nz)
        pl.when(jnp.logical_and(inside, highest(owner) >= s))(lambda: act(owner, highest(owner) - s))

    def line_relay(s):
        def from_line(zo):
            def act(owner, k):
                recv(owner, k)
                for_column(zo, k, start)
            guarded(zo, y, s, act)

        def step(d, carry):
            from_line(z + d)
            from_line(z - d)
            return carry

        lax.fori_loop(1, nz, step, 0)

    def y_relay(s):
        def from_y(zo):
            def act(owner, k):
                recv(owner, k)
                piece(owner, k, core_peer, core_sem.at[k, 1, zo]).start()
            guarded(zo, 1 - y, s, act)

        def step(d, carry):
            from_y(z + d)
            pl.when(d > 0)(lambda: from_y(z - d))
            return carry

        lax.fori_loop(0, nz, step, 0)

    def core_wait(k):
        def step(t, carry):
            owner = t * 2 + (1 - c)
            pl.when(needed(owner, k))(lambda: recv(owner, k))
            return carry
        lax.fori_loop(0, n // 2, step, 0)

    for copy in own_copies:
        copy.wait()
    for s in range(nt - 1):
        def issue(owner, k):
            for_own(k, start)
            for_column(z, k, start)
        guarded(z, y, s, issue)

    load_w.wait()

    def prepare(k, carry):
        wh, wl = split(winv[k])
        w_h[k] = wh
        w_l[k] = wl
        th, tl = split(winv[k].T)
        wtw[k] = mm3(th, tl, wh, wl)
        return carry

    def kid_prepare(kid):
        vh, vl = split(kinv[kid])

        def step(i, carry):
            bh, bl = split(blocks[kid, i])
            value = mm3(bh, bl, vh, vl)
            high = value.astype(BF16)
            kid_h[kid, i] = high
            kid_f[kid, i] = 2.0 * value - high.astype(F32)
            return carry
        lax.fori_loop(0, links, step, 0)

    eye = (
        lax.broadcasted_iota(jnp.int32, (nb, nb), 0)
        == lax.broadcasted_iota(jnp.int32, (nb, nb), 1)
    )

    def set_diagonal(k, value):
        sig_h[k, k], sig_l[k, k] = split(value)
        top_out[k:k + 1, :] = jnp.sum(jnp.where(eye, value, 0.0), axis=0, keepdims=True)

    def column(k):
        after = range(k + 1, nt)

        def scale(r, carry):
            lh, ll = split(pan[k, pl.ds(r * nb, nb), :])
            value = mm3(lh, ll, w_h[k], w_l[k])
            u_h[r], u_l[r] = split(value)
            return carry
        lax.fori_loop(k + 1, nt, scale, 0)

        def row(i):
            total = None
            for j in after:
                term = mm3(sig_h[i, j], sig_l[i, j], u_h[j], u_l[j])
                total = term if total is None else total + term
            return total

        def fill(i, carry):
            value = -row(i)
            sig_h[i, k], sig_l[i, k] = split(value)
            sig_h[k, i], sig_l[k, i] = split(value.T)
            return carry
        lax.fori_loop(k + 1, nt, fill, 0)
        set_diagonal(k, wtw[k] - row(k))

    lax.fori_loop(0, nt, prepare, 0)
    set_diagonal(nt - 1, wtw[nt - 1])
    load_v.wait()
    load_b.wait()
    todo = list(range(kids))
    last = nt - 2
    for s in range(nt - 1):
        k = last - s
        line_relay(s)
        if s >= 1:
            y_relay(s - 1)
        if s >= 2:
            core_wait(k + 2)
            column(k + 2)
        elif todo:
            kid_prepare(todo.pop(0))
    for kid in todo:
        kid_prepare(kid)
    core_wait(1)
    column(1)
    y_relay(last)
    core_wait(0)
    column(0)

    def kid_finish(kid, carry):
        total = jnp.sum(kinv[kid] * kinv[kid], axis=0, keepdims=True)
        for i in range(links):
            coupled = None
            for j in range(links):
                bi, bj = pat[kid, i], pat[kid, j]
                term = mm(sig_h[bi, bj], kid_h[kid, j]) + mm(sig_l[bi, bj], kid_h[kid, j])
                coupled = term if coupled is None else coupled + term
            total = total + jnp.sum(kid_f[kid, i] * coupled, axis=0, keepdims=True)
        kid_out[pl.ds(kid, 1), :] = total
        return carry
    lax.fori_loop(0, kids, kid_finish, 0)

    for k in range(nt - 1):
        pl.when(needed(me, k))(lambda k=k: for_own(k, done))

        def finish(zo, carry, k=k):
            pl.when(needed(index(zo, y, c), k))(lambda: for_column(zo, k, done))

            @pl.when(needed(index(zo, 1 - y, c), k))
            def _():
                piece(index(zo, 1 - y, c), k, core_peer, core_sem.at[k, 1, zo]).wait_send()
            return carry
        lax.fori_loop(0, nz, finish, 0)


def local(n, top_panels, top_inverse, pattern, child_blocks, child_inverse):
    rows = top_panels.shape[0]
    nt, nb = top_inverse.shape[:2]
    kids, links = child_blocks.shape[:2]
    nz = n // 4
    dma = pltpu.SemaphoreType.DMA
    hbm = pl.BlockSpec(memory_space=pl.ANY)
    vmem = pl.BlockSpec(memory_space=pltpu.VMEM)
    diagonal, child_var = pl.pallas_call(
        functools.partial(kernel, n, nt, nb, rows, kids, links),
        out_shape=(
            jax.ShapeDtypeStruct((nt, nb), F32),
            jax.ShapeDtypeStruct((kids, nb), F32),
        ),
        in_specs=[hbm, hbm, pl.BlockSpec(memory_space=pltpu.SMEM), hbm, hbm],
        out_specs=(vmem, vmem),
        scratch_shapes=[
            pltpu.VMEM((nt - 1, nt * nb, nb), F32),
            pltpu.VMEM((nt, nb, nb), F32),
            pltpu.VMEM((kids, links, nb, nb), F32),
            pltpu.VMEM((kids, nb, nb), F32),
            pltpu.VMEM((nt, nb, nb), BF16),
            pltpu.VMEM((nt, nb, nb), BF16),
            pltpu.VMEM((nt, nb, nb), F32),
            pltpu.VMEM((nt, nt, nb, nb), BF16),
            pltpu.VMEM((nt, nt, nb, nb), BF16),
            pltpu.VMEM((nt, nb, nb), BF16),
            pltpu.VMEM((nt, nb, nb), BF16),
            pltpu.VMEM((kids, links, nb, nb), BF16),
            pltpu.VMEM((kids, links, nb, nb), F32),
            dma((nt - 1,)),
            dma((3,)),
            dma((nt - 1, n)),
            dma((nt - 1, nz)),
            dma((nt - 1, nz)),
            dma((nt - 1, nz)),
            dma((nt - 1, 2, nz)),
        ],
        compiler_params=pltpu.CompilerParams(
            collective_id=0, has_side_effects=True, vmem_limit_bytes=60 * 1024 * 1024,
        ),
    )(top_panels, top_inverse, pattern, child_blocks, child_inverse)
    first = lax.axis_index("prow") * rows
    top_var = lax.dynamic_slice_in_dim(diagonal.reshape(nt * nb), first, rows)
    return top_var, child_var


def solution(mesh):
    return jax.shard_map(
        functools.partial(local, mesh.shape["prow"]),
        mesh=mesh,
        in_specs=(
            P(("cfg", "prow"), None),
            P("cfg", None, None),
            P("prow", None),
            P(("cfg", "prow"), None, None, None),
            P(("cfg", "prow"), None, None),
        ),
        out_specs=(P(("cfg", "prow")), P(("cfg", "prow"), None)),
        check_vma=False,
    )
```

```python
import functools

import jax
import jax.numpy as jnp
from jax import lax
from jax.experimental import pallas as pl
from jax.experimental.pallas import tpu as pltpu
from jax.sharding import PartitionSpec as P

F32 = jnp.float32
BF16 = jnp.bfloat16
MESH = pl.DeviceIdType.MESH


def split(x):
    high = x.astype(BF16)
    low = (x - high.astype(F32)).astype(BF16)
    return high, low


def mm(a, b):
    return jnp.dot(a, b, preferred_element_type=F32)


def mm3(ah, al, bh, bl):
    return mm(ah, bh) + mm(ah, bl) + mm(al, bh)


def kernel(
    n, nt, nb, rows, kids, links,
    panels_hbm, winv_hbm, pat, blocks_hbm, kinv_hbm,
    top_out, kid_out,
    pan, winv, blocks, kinv, w_h, w_l, wtw, sig_h, sig_l, u_h, u_l, kid_h, kid_f,
    own_sem, load_sem, recv_sem, line_sem, down_sem, y_sem, core_sem,
):
    cfg = lax.axis_index("cfg")
    me = lax.axis_index("prow")
    nz = n // 4
    z = me // 4
    y = (me // 2) % 2
    c = me % 2

    def index(zo, yo, co):
        return zo * 4 + yo * 2 + co

    y_peer = index(z, 1 - y, c)
    core_peer = index(z, y, 1 - c)
    def needed(owner, k):
        return owner * rows + rows - 1 >= (k + 1) * nb

    own_copies = []
    for k in reversed(range(nt - 1)):
        copy = pltpu.make_async_copy(
            panels_hbm.at[:, k * nb:(k + 1) * nb],
            pan.at[k, pl.ds(me * rows, rows), :],
            own_sem.at[k],
        )
        copy.start()
        own_copies.append(copy)
    load_w = pltpu.make_async_copy(winv_hbm, winv, load_sem.at[0])
    load_v = pltpu.make_async_copy(kinv_hbm, kinv, load_sem.at[1])
    load_b = pltpu.make_async_copy(blocks_hbm, blocks, load_sem.at[2])

    barrier = pltpu.get_barrier_semaphore()
    for peer in (y_peer, core_peer):
        pl.semaphore_signal(barrier, inc=1, device_id=(cfg, peer), device_id_type=MESH)

    def greet(zo, carry):
        @pl.when(zo != z)
        def _():
            pl.semaphore_signal(
                barrier, inc=1, device_id=(cfg, index(zo, y, c)), device_id_type=MESH
            )
        return carry
    lax.fori_loop(0, nz, greet, 0)
    pl.semaphore_wait(barrier, nz + 1)

    def piece(owner, k, peer, sem):
        part = pan.at[k, pl.ds(owner * rows, rows), :]
        return pltpu.make_async_remote_copy(
            src_ref=part, dst_ref=part, send_sem=sem, recv_sem=recv_sem.at[k, owner],
            device_id=(cfg, peer), device_id_type=MESH,
        )

    def recv(owner, k):
        piece(owner, k, core_peer, core_sem.at[k, 0, 0]).wait_recv()

    def for_own(k, act):
        def to_line(zt):
            @pl.when(jnp.logical_and(zt != z, jnp.logical_or(zt > 0, z < 2)))
            def _():
                act(piece(me, k, index(zt, y, c), line_sem.at[k, zt]))

        def step(d, carry):
            pl.when(z - d >= 0)(lambda: to_line(z - d))
            pl.when(z + d < nz)(lambda: to_line(z + d))
            return carry
        lax.fori_loop(1, nz, step, 0)

    def for_column(zo, k, act):
        owner = index(zo, y, c)
        @pl.when(jnp.logical_and(z == 1, zo > 1))
        def _():
            act(piece(owner, k, index(0, y, c), down_sem.at[k, zo]))
        act(piece(owner, k, y_peer, y_sem.at[k, zo]))
        act(piece(owner, k, core_peer, core_sem.at[k, 0, zo]))

    def start(copy):
        copy.start()

    def done(copy):
        copy.wait_send()

    def highest(owner):
        return (owner * rows + rows - 1) // nb - 1

    def guarded(zo, yo, s, act):
        owner = index(zo, yo, c)
        inside = jnp.logical_and(zo >= 0, zo < nz)
        pl.when(jnp.logical_and(inside, highest(owner) >= s))(lambda: act(owner, highest(owner) - s))

    def line_relay(s):
        def from_line(zo):
            def act(owner, k):
                recv(owner, k)
                for_column(zo, k, start)
            guarded(zo, y, s, act)

        def step(d, carry):
            from_line(z + d)
            from_line(z - d)
            return carry

        lax.fori_loop(1, nz, step, 0)

    def y_relay(s):
        def from_y(zo):
            def act(owner, k):
                recv(owner, k)
                piece(owner, k, core_peer, core_sem.at[k, 1, zo]).start()
            guarded(zo, 1 - y, s, act)

        def step(d, carry):
            from_y(z + d)
            pl.when(d > 0)(lambda: from_y(z - d))
            return carry

        lax.fori_loop(0, nz, step, 0)

    def core_wait(k):
        def step(t, carry):
            owner = t * 2 + (1 - c)
            pl.when(needed(owner, k))(lambda: recv(owner, k))
            return carry
        lax.fori_loop(0, n // 2, step, 0)

    for copy in own_copies:
        copy.wait()
    for s in range(nt - 1):
        def issue(owner, k):
            for_own(k, start)
            for_column(z, k, start)
        guarded(z, y, s, issue)

    load_w.start()
    load_v.start()
    load_b.start()
    load_w.wait()

    def prepare(k, carry):
        wh, wl = split(winv[k])
        w_h[k] = wh
        w_l[k] = wl
        th, tl = split(winv[k].T)
        wtw[k] = mm3(th, tl, wh, wl)
        return carry

    def kid_prepare(kid):
        vh, vl = split(kinv[kid])

        def step(i, carry):
            bh, bl = split(blocks[kid, i])
            value = mm3(bh, bl, vh, vl)
            high = value.astype(BF16)
            kid_h[kid, i] = high
            kid_f[kid, i] = 2.0 * value - high.astype(F32)
            return carry
        lax.fori_loop(0, links, step, 0, unroll=True)

    eye = (
        lax.broadcasted_iota(jnp.int32, (nb, nb), 0)
        == lax.broadcasted_iota(jnp.int32, (nb, nb), 1)
    )

    def set_diagonal(k, value):
        sig_h[k, k], sig_l[k, k] = split(value)
        top_out[k:k + 1, :] = jnp.sum(jnp.where(eye, value, 0.0), axis=0, keepdims=True)

    def column(k):
        after = range(k + 1, nt)

        def scale(r, carry):
            lh, ll = split(pan[k, pl.ds(r * nb, nb), :])
            value = mm3(lh, ll, w_h[k], w_l[k])
            u_h[r], u_l[r] = split(value)
            return carry
        lax.fori_loop(k + 1, nt, scale, 0, unroll=True)

        def row(i):
            total = None
            for j in after:
                term = mm3(sig_h[i, j], sig_l[i, j], u_h[j], u_l[j])
                total = term if total is None else total + term
            return total

        def fill(i, carry):
            value = -row(i)
            sig_h[i, k], sig_l[i, k] = split(value)
            sig_h[k, i], sig_l[k, i] = split(value.T)
            return carry
        lax.fori_loop(k + 1, nt, fill, 0, unroll=True)
        set_diagonal(k, wtw[k] - row(k))

    lax.fori_loop(0, nt, prepare, 0)
    set_diagonal(nt - 1, wtw[nt - 1])
    load_v.wait()
    load_b.wait()
    todo = list(range(kids))
    last = nt - 2
    for s in range(nt - 1):
        k = last - s
        line_relay(s)
        if s >= 1:
            y_relay(s - 1)
        if s >= 2:
            core_wait(k + 2)
            column(k + 2)
        elif todo:
            kid_prepare(todo.pop(0))
    for kid in todo:
        kid_prepare(kid)
    y_relay(last)
    core_wait(1)
    column(1)
    core_wait(0)
    column(0)

    def kid_finish(kid, carry):
        total = jnp.sum(kinv[kid] * kinv[kid], axis=0, keepdims=True)
        for i in range(links):
            coupled = None
            for j in range(links):
                bi, bj = pat[kid, i], pat[kid, j]
                term = mm(sig_h[bi, bj], kid_h[kid, j]) + mm(sig_l[bi, bj], kid_h[kid, j])
                coupled = term if coupled is None else coupled + term
            total = total + jnp.sum(kid_f[kid, i] * coupled, axis=0, keepdims=True)
        kid_out[pl.ds(kid, 1), :] = total
        return carry
    lax.fori_loop(0, kids, kid_finish, 0)

    for k in range(nt - 1):
        pl.when(needed(me, k))(lambda k=k: for_own(k, done))

        def finish(zo, carry, k=k):
            pl.when(needed(index(zo, y, c), k))(lambda: for_column(zo, k, done))

            @pl.when(needed(index(zo, 1 - y, c), k))
            def _():
                piece(index(zo, 1 - y, c), k, core_peer, core_sem.at[k, 1, zo]).wait_send()
            return carry
        lax.fori_loop(0, nz, finish, 0)


def local(n, top_panels, top_inverse, pattern, child_blocks, child_inverse):
    rows = top_panels.shape[0]
    nt, nb = top_inverse.shape[:2]
    kids, links = child_blocks.shape[:2]
    nz = n // 4
    dma = pltpu.SemaphoreType.DMA
    hbm = pl.BlockSpec(memory_space=pl.ANY)
    vmem = pl.BlockSpec(memory_space=pltpu.VMEM)
    diagonal, child_var = pl.pallas_call(
        functools.partial(kernel, n, nt, nb, rows, kids, links),
        out_shape=(
            jax.ShapeDtypeStruct((nt, nb), F32),
            jax.ShapeDtypeStruct((kids, nb), F32),
        ),
        in_specs=[hbm, hbm, pl.BlockSpec(memory_space=pltpu.SMEM), hbm, hbm],
        out_specs=(vmem, vmem),
        scratch_shapes=[
            pltpu.VMEM((nt - 1, nt * nb, nb), F32),
            pltpu.VMEM((nt, nb, nb), F32),
            pltpu.VMEM((kids, links, nb, nb), F32),
            pltpu.VMEM((kids, nb, nb), F32),
            pltpu.VMEM((nt, nb, nb), BF16),
            pltpu.VMEM((nt, nb, nb), BF16),
            pltpu.VMEM((nt, nb, nb), F32),
            pltpu.VMEM((nt, nt, nb, nb), BF16),
            pltpu.VMEM((nt, nt, nb, nb), BF16),
            pltpu.VMEM((nt, nb, nb), BF16),
            pltpu.VMEM((nt, nb, nb), BF16),
            pltpu.VMEM((kids, links, nb, nb), BF16),
            pltpu.VMEM((kids, links, nb, nb), F32),
            dma((nt - 1,)),
            dma((3,)),
            dma((nt - 1, n)),
            dma((nt - 1, nz)),
            dma((nt - 1, nz)),
            dma((nt - 1, nz)),
            dma((nt - 1, 2, nz)),
        ],
        compiler_params=pltpu.CompilerParams(
            collective_id=0, has_side_effects=True, vmem_limit_bytes=60 * 1024 * 1024,
        ),
    )(top_panels, top_inverse, pattern, child_blocks, child_inverse)
    first = lax.axis_index("prow") * rows
    top_var = lax.dynamic_slice_in_dim(diagonal.reshape(nt * nb), first, rows)
    return top_var, child_var


def solution(mesh):
    return jax.shard_map(
        functools.partial(local, mesh.shape["prow"]),
        mesh=mesh,
        in_specs=(
            P(("cfg", "prow"), None),
            P("cfg", None, None),
            P("prow", None),
            P(("cfg", "prow"), None, None, None),
            P(("cfg", "prow"), None, None),
        ),
        out_specs=(P(("cfg", "prow")), P(("cfg", "prow"), None)),
        check_vma=False,
    )
```
